32 devices in a mesh: row: 8 (over y, x, core), col: 4 (over z).
Axes of the slice: x: 2, y: 2, z: 4, core: 2. Of those that a mesh axis runs over, the one named last changes fastest.
Arguments:
- b_ingest: bfloat16 [65536, 1024], P(('row', 'col')), may hold values from -6 to 6
- source_point: int32 [65536], P(('row', 'col')), may hold values from 0 to 65535, as said below
- panels: bfloat16 [2, 8, 8, 1024, 1024], P(None, None, 'row', 'col'), may hold values from -0.1875 to 0.1875
- diag_inverse: bfloat16 [2, 1024, 1024], replicated, may hold values from -1 to 1.5, as said below
Outputs:
- updated: bfloat16 [8, 8, 1024, 1024], P(None, 'row', 'col')
The draws below stay inside these ranges and needn't reach their ends.
Inputs may be any that keep to these rules, and one draw needn't show every extreme that they name: source_point is a permutation of 0 to 65535. Say point i lies in block b = i // 1024 at offset o = i mod 1024; it belongs to the device with row index b mod 8 and col index o // (1024 / 4). The shard of source_point on each device along row+col holds exactly 64 points of every device. diag_inverse[k] is lower triangular with diagonal entries between 0.5 and 1.5.
All inputs are finite; a program needn't handle non-finite values.
Results may differ from the reference program's by a relative error of at most 0.0056.
Values may be sent and summed in bfloat16 or wider, within the bound.
A program may use at most 64 MiB of HBM per device.

```python
import jax
import jax.numpy as jnp
from jax import lax

PANEL_WIDTH = 1024
DRAW_COUNT = 1024
LOCAL_BLOCKS = 8
POINTS = 65536
N_ROW = 8
N_COL = 4


def draw_source_point(key, part):
    row_count = N_ROW
    col_count = N_COL
    dev_count = row_count * col_count
    per_device = POINTS // dev_count
    per_peer = per_device // dev_count
    block_rows = PANEL_WIDTH // col_count
    device_ids = jnp.arange(dev_count, dtype=jnp.int32)[:, None]
    local_ids = jnp.arange(per_device, dtype=jnp.int32)[None, :]
    grid_row = device_ids // col_count
    grid_col = device_ids % col_count
    local_block = local_ids // block_rows
    offset = local_ids % block_rows
    points = (local_block * row_count + grid_row) * PANEL_WIDTH + grid_col * block_rows + offset
    first_key = jax.random.fold_in(key, 11)
    second_key = jax.random.fold_in(key, 23)
    points = jax.random.permutation(first_key, points, axis=1, independent=True)
    points = points.reshape(dev_count, dev_count, per_peer)
    points = jnp.transpose(points, (1, 0, 2)).reshape(dev_count, per_device)
    points = jax.random.permutation(second_key, points, axis=1, independent=True)
    return points.reshape(POINTS).astype(jnp.int32)


def draw_diag_inverse(key, part):
    off_key = jax.random.fold_in(key, 5)
    diag_key = jax.random.fold_in(key, 7)
    lower = jax.random.truncated_normal(off_key, -6.0, 6.0, (2, PANEL_WIDTH, PANEL_WIDTH), jnp.float32) * PANEL_WIDTH ** (-0.5)
    diagonal = jax.random.uniform(diag_key, (2, PANEL_WIDTH, 1), jnp.float32, 0.5, 1.5)
    row_ids = jnp.arange(PANEL_WIDTH, dtype=jnp.int32)[:, None]
    col_ids = jnp.arange(PANEL_WIDTH, dtype=jnp.int32)[None, :]
    below = (row_ids > col_ids)[None, :, :]
    on_diag = (row_ids == col_ids)[None, :, :]
    value = jnp.where(below, lower, 0.0) + jnp.where(on_diag, diagonal, 0.0)
    return value.astype(jnp.bfloat16)


def block_scale(rng, extent, cuts, smallest, largest):
    factor_of, own = 1.0, jax.random.fold_in(rng, 6)
    for position, blocks in cuts:
        heights = jnp.exp(jax.random.uniform(jax.random.fold_in(own, position), (blocks,), jnp.float32, smallest / len(cuts), largest / len(cuts)))
        factor_of = factor_of * jnp.repeat(heights, extent[position] // blocks).reshape([-1 if axis == position else 1 for axis in range(len(extent))])
    return factor_of


def centred(stream_key, dims, spread, reach, split=(), kind=jnp.bfloat16):
    entries = spread * jax.random.normal(stream_key, dims, jnp.float32)
    if split:
        entries = entries * block_scale(stream_key, dims, split, -0.22, 0.18)
    return jnp.clip(entries, -reach, reach).astype(kind)


def setup_inputs(seed: int = 0) -> dict:
    streams_of = jax.random.split(jax.random.key(seed), 5)
    b_ingest = centred(streams_of[0], (POINTS, DRAW_COUNT), 1.0, 6.0, ((0, 32),))
    source_point = draw_source_point(jax.random.fold_in(streams_of[4], 71), 0)
    panels = centred(streams_of[2], (2, LOCAL_BLOCKS, N_ROW, PANEL_WIDTH, PANEL_WIDTH), PANEL_WIDTH ** -0.5, 0.1875, ((2, 8), (3, 4)))
    diag_inverse = draw_diag_inverse(jax.random.fold_in(streams_of[4], 71), 0)
    return {"b_ingest": b_ingest, "source_point": source_point, "panels": panels, "diag_inverse": diag_inverse}


def reference(b_ingest, source_point, panels, diag_inverse):
    rhs = jnp.zeros((POINTS, DRAW_COUNT), jnp.bfloat16).at[source_point].set(b_ingest)
    blocks = rhs.reshape(LOCAL_BLOCKS * N_ROW, PANEL_WIDTH, DRAW_COUNT)
    factor = panels.reshape(2, LOCAL_BLOCKS * N_ROW, PANEL_WIDTH, PANEL_WIDTH)
    solved0 = jnp.dot(diag_inverse[0].astype(jnp.float32), blocks[0].astype(jnp.float32)).astype(jnp.bfloat16)
    second = (blocks[1].astype(jnp.float32) - jnp.dot(factor[0, 1].astype(jnp.float32), solved0.astype(jnp.float32))).astype(jnp.bfloat16)
    solved1 = jnp.dot(diag_inverse[1].astype(jnp.float32), second.astype(jnp.float32)).astype(jnp.bfloat16)
    first_f = solved0.astype(jnp.float32)
    second_f = solved1.astype(jnp.float32)

    def one_block(items):
        block_rhs, factor0, factor1 = items
        value = block_rhs.astype(jnp.float32) - jnp.dot(factor0.astype(jnp.float32), first_f)
        value = value - jnp.dot(factor1.astype(jnp.float32), second_f)
        return value.astype(jnp.bfloat16)

    result = lax.map(one_block, (blocks, factor[0], factor[1]))
    result = result.at[0].set(solved0).at[1].set(solved1)
    return result.reshape(LOCAL_BLOCKS, N_ROW, PANEL_WIDTH, DRAW_COUNT)
```

```python
import functools

import jax
import jax.numpy as jnp
from jax import lax
from jax.experimental import pallas as pl
from jax.experimental.pallas import tpu as pltpu
from jax.sharding import PartitionSpec as P

MESH = pl.DeviceIdType.MESH
BF16 = jnp.bfloat16
F32 = jnp.float32
GROUP = 256


def broadcast(block, axis, owner):
    block = jnp.where(lax.axis_index(axis) == owner, block, jnp.zeros_like(block))
    return lax.psum(block, axis)


def plain_per_device(b_ingest, source_point, panels, diag_inverse):
    row_count = lax.axis_size("row")
    col_count = lax.axis_size("col")
    dev_count = row_count * col_count
    block_rows = panels.shape[3]
    panel_width = panels.shape[4]
    local_count = panels.shape[1]
    rows_dev = local_count * block_rows
    draw_count = b_ingest.shape[1]
    per_peer = rows_dev // dev_count
    owner_block = source_point // panel_width
    target = owner_block % row_count * col_count + source_point % panel_width // block_rows
    sort_keys = target * rows_dev + jnp.arange(rows_dev, dtype=jnp.int32)
    ordering = jnp.argsort(sort_keys)
    ordered = b_ingest[ordering]
    ordered_ids = source_point[ordering]
    arrived, arrived_ids = (
        lax.all_to_all(
            ordered.reshape(dev_count, per_peer, draw_count),
            ("row", "col"),
            split_axis=0,
            concat_axis=0,
            tiled=True,
        ),
        lax.all_to_all(
            ordered_ids.reshape(dev_count, per_peer),
            ("row", "col"),
            split_axis=0,
            concat_axis=0,
            tiled=True,
        ),
    )
    arrived = arrived.reshape(rows_dev, draw_count)
    arrived_ids = arrived_ids.reshape(rows_dev)
    arrived_block = arrived_ids // panel_width
    local_row = arrived_block // row_count * block_rows + arrived_ids % panel_width % block_rows
    resident = jnp.zeros((rows_dev, draw_count), jnp.bfloat16).at[local_row].set(arrived)
    running = resident.astype(jnp.float32)
    row_id = lax.axis_index("row")
    col_id = lax.axis_index("col")
    global_block = jnp.arange(rows_dev, dtype=jnp.int32) // block_rows * row_count + row_id
    solved = []
    for panel_index in range(2):
        factor_rows = panels[panel_index].reshape(rows_dev, panel_width)
        inverse = diag_inverse[panel_index]
        leading = running[:block_rows].astype(jnp.bfloat16)
        shared = broadcast(leading, "row", panel_index)
        full_solved = jnp.dot(
            inverse,
            lax.all_gather(shared, "col", axis=0, tiled=True),
            preferred_element_type=jnp.float32,
        ).astype(jnp.bfloat16)
        update = jnp.dot(factor_rows, full_solved, preferred_element_type=jnp.float32)
        own_solved = lax.dynamic_slice_in_dim(full_solved, col_id * block_rows, block_rows, 0)
        running = running - jnp.where((global_block > panel_index)[:, None], update, 0.0)
        solved.append(own_solved)
    result = running.astype(jnp.bfloat16)
    head_rows = result[:block_rows]
    head_rows = jnp.where(row_id == 0, solved[0], jnp.where(row_id == 1, solved[1], head_rows))
    result = jnp.concatenate([head_rows, result[block_rows:]], axis=0)
    return result.reshape(local_count, 1, block_rows, draw_count)


def dot(a, b):
    return jnp.dot(a, b, preferred_element_type=F32)


def kernel(
    R, C, panel_width, id_ref, b_ref, pan_hbm, diag_hbm, out_ref,
    bs, rv, ids_s, ids_r, rank_ref, lr_ref, pan, dg, H, sol, acc,
    local_sem, self_sem, s_send, s_recv, i_send, i_recv, a_send, b_send, c_send, d_send, p_recv, d_recv,
):
    D = R * C
    rows_dev, draws = b_ref.shape
    per_peer = rows_dev // D
    L = pan.shape[1]
    block_rows = pan.shape[2]
    nq = R // 2
    sub = block_rows // nq
    in_group = GROUP // per_peer
    groups = rows_dev // GROUP
    row = lax.axis_index("row")
    col = lax.axis_index("col")
    me = row * C + col
    core = lax.rem(row, 2)
    quarter = lax.div(row, 2)
    sibling = row + 1 - 2 * core

    pan_copy = pltpu.make_async_copy(pan_hbm.at[:, :, 0], pan, local_sem.at[0])
    diag_copy = pltpu.make_async_copy(diag_hbm, dg, local_sem.at[1])
    pan_copy.start()
    diag_copy.start()

    barrier = pltpu.get_barrier_semaphore()

    def greet(i, _):
        peer = lax.rem(me + i, D)
        pl.semaphore_signal(barrier, inc=1, device_id=(lax.div(peer, C), lax.rem(peer, C)), device_id_type=MESH)
        return 0

    lax.fori_loop(1, D, greet, 0)

    ids = id_ref[...]
    block = lax.div(ids, panel_width)
    offset = ids - block * panel_width
    local_block = lax.div(block, R)
    target_col = lax.div(offset, block_rows)
    target = (block - local_block * R) * C + target_col
    local_row = local_block * block_rows + offset - target_col * block_rows
    hits = jnp.where(lax.broadcasted_iota(jnp.int32, (D, rows_dev), 0) == target, 1.0, 0.0)
    chunks = [hits[:, g * GROUP:(g + 1) * GROUP] for g in range(groups)]
    upper = jnp.where(
        lax.broadcasted_iota(jnp.int32, (GROUP, GROUP), 0) < lax.broadcasted_iota(jnp.int32, (GROUP, GROUP), 1), 1.0, 0.0
    ).astype(BF16)
    before = dot(jnp.concatenate(chunks, axis=0).astype(BF16), upper)
    carry = jnp.zeros((D, 1), F32)
    for g in range(groups):
        part = chunks[g] * (before[g * D:(g + 1) * D] + carry)
        rank_ref[:, g * GROUP:(g + 1) * GROUP] = jnp.sum(part, axis=0, keepdims=True).astype(jnp.int32)
        carry = carry + jnp.sum(chunks[g], axis=1, keepdims=True)
    rank = rank_ref[...]
    place = target * per_peer + rank
    high = lax.div(local_row, 64)
    low = local_row - high * 64
    coded = jnp.concatenate([hits * high.astype(F32), hits * low.astype(F32)], axis=0).astype(BF16)
    lane = rank + lax.rem(me, in_group) * per_peer
    spread = jnp.where(lax.broadcasted_iota(jnp.int32, (GROUP, rows_dev), 0) == lane, 1.0, 0.0).astype(BF16)
    sent_ids = lax.dot_general(coded, spread, (((1,), (1,)), ((), ())), preferred_element_type=F32)
    sent_ids = (sent_ids[:D] * 64.0 + sent_ids[D:]).astype(jnp.int32)
    for t in range(D):
        ids_s[t] = sent_ids[t:t + 1]
    rank_ref[...] = place

    pl.semaphore_wait(barrier, D - 1)

    def row_copy(t, slot):
        return pltpu.make_async_remote_copy(
            src_ref=bs.at[t], dst_ref=rv.at[slot], send_sem=s_send.at[t], recv_sem=s_recv.at[slot],
            device_id=(lax.div(t, C), lax.rem(t, C)), device_id_type=MESH)

    def id_copy(t, slot):
        return pltpu.make_async_remote_copy(
            src_ref=ids_s.at[t], dst_ref=ids_r.at[slot], send_sem=i_send.at[t], recv_sem=i_recv.at[slot],
            device_id=(lax.div(t, C), lax.rem(t, C)), device_id_type=MESH)

    own_rows = pltpu.make_async_copy(bs.at[me], rv.at[me], self_sem.at[0])
    own_ids = pltpu.make_async_copy(ids_s.at[me], ids_r.at[me], self_sem.at[1])

    def send_group(i, _):
        g = jnp.where(i < 2, i, 2 + lax.rem(i + row, R - 2))
        slots = lax.broadcasted_iota(jnp.int32, (C * per_peer, rows_dev), 0) + g * (C * per_peer)
        pick = jnp.where(slots == rank_ref[...], 1.0, 0.0).astype(BF16)
        picked = dot(pick, b_ref[...]).astype(BF16)
        bs[pl.ds(g * C, C)] = picked.reshape(C, per_peer, draws)

        def send(j, _):
            t = g * C + lax.rem(col + j, C)

            @pl.when(t != me)
            def _():
                id_copy(t, me).start()
                row_copy(t, me).start()

            @pl.when(t == me)
            def _():
                own_ids.start()
                own_rows.start()

            return 0

        lax.fori_loop(0, C, send, 0)
        return 0

    lax.fori_loop(0, R, send_group, 0)

    def wait_arrived():
        def wait_one(i, _):
            s = lax.rem(me + i, D)
            id_copy(s, s).wait_recv()
            row_copy(s, s).wait_recv()
            return 0

        lax.fori_loop(1, D, wait_one, 0)
        own_ids.wait()
        own_rows.wait()
        for g in range(groups):
            ids_g = ids_r[g * in_group]
            for i in range(1, in_group):
                ids_g = ids_g + ids_r[g * in_group + i]
            lr_ref[:, g * GROUP:(g + 1) * GROUP] = ids_g

    def placed(first, count):
        slots = lax.broadcasted_iota(jnp.int32, (count, rows_dev), 0) + first
        put = jnp.where(slots == lr_ref[...], 1.0, 0.0).astype(BF16)
        return dot(put, rv[...].reshape(rows_dev, draws))

    def piece(k, c, q, send_sem, to_row, to_col):
        return pltpu.make_async_remote_copy(
            src_ref=H.at[k, c, q], dst_ref=H.at[k, c, q], send_sem=send_sem, recv_sem=p_recv.at[k, c, q],
            device_id=(to_row, to_col), device_id_type=MESH)

    def slab(k, c):
        return pltpu.make_async_remote_copy(
            src_ref=H.at[k, c], dst_ref=H.at[k, c], send_sem=d_send.at[c], recv_sem=d_recv.at[k, c],
            device_id=(sibling, col), device_id_type=MESH)

    def share(k):
        @pl.when(row == k)
        def _():
            for q in range(1, nq):
                piece(k, col, q, a_send.at[q], 2 * q + k, col).start()

        @pl.when(core == k)
        def _():
            @pl.when(row != k)
            def _():
                piece(k, col, quarter, a_send.at[0], sibling, col).wait_recv()

            for i in range(1, C):
                other = lax.rem(col + i, C)
                piece(k, col, quarter, b_send.at[i], row, other).start()
            for i in range(C):
                c = lax.rem(col + i, C)
                if i:
                    piece(k, c, quarter, b_send.at[i], sibling, col).wait_recv()
                for j in range(1, nq):
                    q = lax.rem(quarter + j, nq)

                    def go(c=c, q=q, i=i, j=j):
                        piece(k, c, quarter, c_send.at[i, j], 2 * q + k, col).start()

                    if i:
                        go()
                    else:
                        pl.when(q != 0)(go)
            for i in range(C):
                c = lax.rem(col + i, C)
                for j in range(1, nq):
                    q = lax.rem(quarter + j, nq)

                    def take(c=c, q=q):
                        piece(k, c, q, a_send.at[0], sibling, col).wait_recv()

                    if i:
                        take()
                    else:
                        pl.when(row != k)(take)
                slab(k, c).start()

        @pl.when(core != k)
        def _():
            for c in range(C):
                slab(k, c).wait_recv()

    def settle(k):
        @pl.when(row == k)
        def _():
            for q in range(1, nq):
                piece(k, col, q, a_send.at[q], 2 * q + k, col).wait_send()

        @pl.when(core == k)
        def _():
            for i in range(1, C):
                piece(k, col, quarter, b_send.at[i], row, col).wait_send()
            for i in range(C):
                for j in range(1, nq):
                    q = lax.rem(quarter + j, nq)

                    def done(i=i, j=j):
                        piece(k, col, quarter, c_send.at[i, j], sibling, col).wait_send()

                    if i:
                        done()
                    else:
                        pl.when(q != 0)(done)
                slab(k, lax.rem(col + i, C)).wait_send()

    def solve(k):
        whole = H[k].reshape(panel_width, draws)

        def step(i, _):
            at = pl.ds(pl.multiple_of(i * GROUP, GROUP), GROUP)
            sol[k, at, :] = dot(dg[k, at, :], whole).astype(BF16)
            return 0

        lax.fori_loop(0, panel_width // GROUP, step, 0)

    @pl.when(row < 2)
    def _():
        wait_arrived()

    @pl.when(row == 0)
    def _():
        H[0, col] = placed(0, block_rows).astype(BF16).reshape(nq, sub, draws)

    share(0)
    diag_copy.wait()
    solve(0)
    pan_copy.wait()

    @pl.when(row == 1)
    def _():
        second = placed(0, block_rows) - dot(pan[0, 0], sol[0])
        H[1, col] = second.astype(BF16).reshape(nq, sub, draws)

    share(1)
    solve(1)

    def trailing(i, _):
        acc[i] = dot(pan[0, i], sol[0]) + dot(pan[1, i], sol[1])
        return 0

    lax.fori_loop(0, L, trailing, 0)

    @pl.when(row >= 2)
    def _():
        wait_arrived()

    def finish(i, _):
        out_ref[i] = (placed(i * block_rows, block_rows) - acc[i]).astype(BF16)
        return 0

    lax.fori_loop(0, L, finish, 0)
    own = pl.ds(pl.multiple_of(col * block_rows, block_rows), block_rows)
    for k in range(2):
        @pl.when(row == k)
        def _(k=k):
            out_ref[0] = sol[k, own, :]

    def sent(i, _):
        t = lax.rem(me + i, D)
        id_copy(t, me).wait_send()
        row_copy(t, me).wait_send()
        return 0

    lax.fori_loop(1, D, sent, 0)
    settle(0)
    settle(1)


def kernel_per_device(b_ingest, source_point, panels, diag_inverse):
    R, C = lax.axis_size("row"), lax.axis_size("col")
    D = R * C
    _, L, _, block_rows, panel_width = panels.shape
    rows_dev, draws = b_ingest.shape
    per_peer = rows_dev // D
    nq = R // 2
    dma = pltpu.SemaphoreType.DMA
    vmem = pl.BlockSpec(memory_space=pltpu.VMEM)
    hbm = pl.BlockSpec(memory_space=pl.ANY)
    out = pl.pallas_call(
        functools.partial(kernel, R, C, panel_width),
        out_shape=jax.ShapeDtypeStruct((L, block_rows, draws), BF16),
        in_specs=[vmem, vmem, hbm, hbm],
        out_specs=vmem,
        scratch_shapes=[
            pltpu.VMEM((D, per_peer, draws), BF16),
            pltpu.VMEM((D, per_peer, draws), BF16),
            pltpu.VMEM((D, 1, GROUP), jnp.int32),
            pltpu.VMEM((D, 1, GROUP), jnp.int32),
            pltpu.VMEM((1, rows_dev), jnp.int32),
            pltpu.VMEM((1, rows_dev), jnp.int32),
            pltpu.VMEM((2, L, block_rows, panel_width), BF16),
            pltpu.VMEM((2, panel_width, panel_width), BF16),
            pltpu.VMEM((2, C, nq, block_rows // nq, draws), BF16),
            pltpu.VMEM((2, panel_width, draws), BF16),
            pltpu.VMEM((L, block_rows, draws), F32),
            dma((2,)),
            dma((2,)),
            dma((D,)),
            dma((D,)),
            dma((D,)),
            dma((D,)),
            dma((nq,)),
            dma((C,)),
            dma((C, nq)),
            dma((C,)),
            dma((2, C, nq)),
            dma((2, C)),
        ],
        compiler_params=pltpu.CompilerParams(
            collective_id=0, has_side_effects=True, vmem_limit_bytes=60 * 1024 * 1024
        ),
        cost_estimate=pl.CostEstimate(
            flops=4 * rows_dev * panel_width * draws * 2, bytes_accessed=20 * 1024 * 1024, transcendentals=0
        ),
    )(source_point.reshape(1, rows_dev), b_ingest, panels, diag_inverse)
    return out.reshape(L, 1, block_rows, draws)


def per_device(b_ingest, source_point, panels, diag_inverse):
    R, C = lax.axis_size("row"), lax.axis_size("col")
    rows_dev, draws = b_ingest.shape
    block_rows, panel_width = panels.shape[3:]
    per_peer = rows_dev // (R * C)
    fits = (
        R % 2 == 0 and R > 3 and C > 1
        and per_peer % 16 == 0 and GROUP % per_peer == 0
        and rows_dev % GROUP == 0 and panel_width % GROUP == 0
        and block_rows % (R // 2 * 16) == 0 and rows_dev <= 64 * 256
        and rows_dev * (12 * draws + 4 * panel_width) + panel_width * (4 * panel_width + 8 * draws) <= 48 * 1024 * 1024
    )
    body = kernel_per_device if fits else plain_per_device
    return body(b_ingest, source_point, panels, diag_inverse)


def solution(mesh):
    return jax.shard_map(
        per_device,
        mesh=mesh,
        in_specs=(
            P(("row", "col"), None),
            P(("row", "col")),
            P(None, None, "row", "col", None),
            P(),
        ),
        out_specs=P(None, "row", "col", None),
        check_vma=False,
    )
```

```python
import functools

import jax
import jax.numpy as jnp
from jax import lax
from jax.experimental import pallas as pl
from jax.experimental.pallas import tpu as pltpu
from jax.sharding import PartitionSpec as P

MESH = pl.DeviceIdType.MESH
BF16 = jnp.bfloat16
F32 = jnp.float32
GROUP = 256


def broadcast(block, axis, owner):
    block = jnp.where(lax.axis_index(axis) == owner, block, jnp.zeros_like(block))
    return lax.psum(block, axis)


def plain_per_device(b_ingest, source_point, panels, diag_inverse):
    row_count = lax.axis_size("row")
    col_count = lax.axis_size("col")
    dev_count = row_count * col_count
    block_rows = panels.shape[3]
    panel_width = panels.shape[4]
    local_count = panels.shape[1]
    rows_dev = local_count * block_rows
    draw_count = b_ingest.shape[1]
    per_peer = rows_dev // dev_count
    owner_block = source_point // panel_width
    target = owner_block % row_count * col_count + source_point % panel_width // block_rows
    sort_keys = target * rows_dev + jnp.arange(rows_dev, dtype=jnp.int32)
    ordering = jnp.argsort(sort_keys)
    ordered = b_ingest[ordering]
    ordered_ids = source_point[ordering]
    arrived, arrived_ids = (
        lax.all_to_all(
            ordered.reshape(dev_count, per_peer, draw_count),
            ("row", "col"),
            split_axis=0,
            concat_axis=0,
            tiled=True,
        ),
        lax.all_to_all(
            ordered_ids.reshape(dev_count, per_peer),
            ("row", "col"),
            split_axis=0,
            concat_axis=0,
            tiled=True,
        ),
    )
    arrived = arrived.reshape(rows_dev, draw_count)
    arrived_ids = arrived_ids.reshape(rows_dev)
    arrived_block = arrived_ids // panel_width
    local_row = arrived_block // row_count * block_rows + arrived_ids % panel_width % block_rows
    resident = jnp.zeros((rows_dev, draw_count), jnp.bfloat16).at[local_row].set(arrived)
    running = resident.astype(jnp.float32)
    row_id = lax.axis_index("row")
    col_id = lax.axis_index("col")
    global_block = jnp.arange(rows_dev, dtype=jnp.int32) // block_rows * row_count + row_id
    solved = []
    for panel_index in range(2):
        factor_rows = panels[panel_index].reshape(rows_dev, panel_width)
        inverse = diag_inverse[panel_index]
        leading = running[:block_rows].astype(jnp.bfloat16)
        shared = broadcast(leading, "row", panel_index)
        full_solved = jnp.dot(
            inverse,
            lax.all_gather(shared, "col", axis=0, tiled=True),
            preferred_element_type=jnp.float32,
        ).astype(jnp.bfloat16)
        update = jnp.dot(factor_rows, full_solved, preferred_element_type=jnp.float32)
        own_solved = lax.dynamic_slice_in_dim(full_solved, col_id * block_rows, block_rows, 0)
        running = running - jnp.where((global_block > panel_index)[:, None], update, 0.0)
        solved.append(own_solved)
    result = running.astype(jnp.bfloat16)
    head_rows = result[:block_rows]
    head_rows = jnp.where(row_id == 0, solved[0], jnp.where(row_id == 1, solved[1], head_rows))
    result = jnp.concatenate([head_rows, result[block_rows:]], axis=0)
    return result.reshape(local_count, 1, block_rows, draw_count)


PLAN = (0, 8, 4)


def dot(a, b):
    return jnp.dot(a, b, preferred_element_type=F32)


def kernel(
    R, C, panel_width, plan, id_ref, b_ref, pan_hbm, diag_hbm, out_ref,
    bs, rv, ids_s, ids_r, rank_ref, lr_ref, pan, dg, H, sol, sec, fac, acc,
    local_sem, self_sem, s_send, s_recv, i_send, i_recv, a_send, b_send, c_send, d_send, p_recv, d_recv,
):
    D = R * C
    rows_dev, draws = b_ref.shape
    per_peer = rows_dev // D
    L = pan.shape[1]
    block_rows = pan.shape[2]
    nq = R // 2
    sub = block_rows // nq
    in_group = GROUP // per_peer
    groups = rows_dev // GROUP
    row = lax.axis_index("row")
    col = lax.axis_index("col")
    me = row * C + col
    core = lax.rem(row, 2)
    quarter = lax.div(row, 2)
    sibling = row + 1 - 2 * core

    pan_copy = pltpu.make_async_copy(pan_hbm.at[:, :, 0], pan, local_sem.at[0])
    diag_copy = pltpu.make_async_copy(diag_hbm, dg, local_sem.at[1])
    pan_copy.start()
    diag_copy.start()

    barrier = pltpu.get_barrier_semaphore()

    def greet(i, _):
        peer = lax.rem(me + i, D)
        pl.semaphore_signal(barrier, inc=1, device_id=(lax.div(peer, C), lax.rem(peer, C)), device_id_type=MESH)
        return 0

    lax.fori_loop(1, D, greet, 0)

    ids = id_ref[...]
    block = lax.div(ids, panel_width)
    offset = ids - block * panel_width
    local_block = lax.div(block, R)
    target_col = lax.div(offset, block_rows)
    target = (block - local_block * R) * C + target_col
    local_row = local_block * block_rows + offset - target_col * block_rows
    hits = jnp.where(lax.broadcasted_iota(jnp.int32, (D, rows_dev), 0) == target, 1.0, 0.0)
    chunks = [hits[:, g * GROUP:(g + 1) * GROUP] for g in range(groups)]
    upper = jnp.where(
        lax.broadcasted_iota(jnp.int32, (GROUP, GROUP), 0) < lax.broadcasted_iota(jnp.int32, (GROUP, GROUP), 1), 1.0, 0.0
    ).astype(BF16)
    before = dot(jnp.concatenate(chunks, axis=0).astype(BF16), upper)
    carry = jnp.zeros((D, 1), F32)
    for g in range(groups):
        part = chunks[g] * (before[g * D:(g + 1) * D] + carry)
        rank_ref[:, g * GROUP:(g + 1) * GROUP] = jnp.sum(part, axis=0, keepdims=True).astype(jnp.int32)
        carry = carry + jnp.sum(chunks[g], axis=1, keepdims=True)
    rank = rank_ref[...]
    place = target * per_peer + rank
    high = lax.div(local_row, 64)
    low = local_row - high * 64
    coded = jnp.concatenate([hits * high.astype(F32), hits * low.astype(F32)], axis=0).astype(BF16)
    lane = rank + lax.rem(me, in_group) * per_peer
    spread = jnp.where(lax.broadcasted_iota(jnp.int32, (GROUP, rows_dev), 0) == lane, 1.0, 0.0).astype(BF16)
    sent_ids = lax.dot_general(coded, spread, (((1,), (1,)), ((), ())), preferred_element_type=F32)
    sent_ids = (sent_ids[:D] * 64.0 + sent_ids[D:]).astype(jnp.int32)
    for t in range(D):
        ids_s[t] = sent_ids[t:t + 1]
    rank_ref[...] = place

    pl.semaphore_wait(barrier, D - 1)

    def row_copy(t, slot):
        return pltpu.make_async_remote_copy(
            src_ref=bs.at[t], dst_ref=rv.at[slot], send_sem=s_send.at[t], recv_sem=s_recv.at[slot],
            device_id=(lax.div(t, C), lax.rem(t, C)), device_id_type=MESH)

    def id_copy(t, slot):
        return pltpu.make_async_remote_copy(
            src_ref=ids_s.at[t], dst_ref=ids_r.at[slot], send_sem=i_send.at[t], recv_sem=i_recv.at[slot],
            device_id=(lax.div(t, C), lax.rem(t, C)), device_id_type=MESH)

    own_rows = pltpu.make_async_copy(bs.at[me], rv.at[me], self_sem.at[0])
    own_ids = pltpu.make_async_copy(ids_s.at[me], ids_r.at[me], self_sem.at[1])

    def group_of(i):
        return jnp.where(i < 2, i, 2 + lax.rem(i + row, R - 2))

    def pick_group(i, _):
        g = group_of(i)
        slots = lax.broadcasted_iota(jnp.int32, (C * per_peer, rows_dev), 0) + g * (C * per_peer)
        pick = jnp.where(slots == rank_ref[...], 1.0, 0.0).astype(BF16)
        picked = dot(pick, b_ref[...]).astype(BF16)
        bs[pl.ds(g * C, C)] = picked.reshape(C, per_peer, draws)
        return 0

    def send_one(n, _):
        t = group_of(lax.div(n, C)) * C + lax.rem(col + n, C)

        @pl.when(t != me)
        def _():
            id_copy(t, me).start()
            row_copy(t, me).start()

        @pl.when(t == me)
        def _():
            own_ids.start()
            own_rows.start()

        return 0

    def send_until(first, last):
        last = min(last, D)
        if first < last:
            lax.fori_loop(first, last, send_one, 0)
        return max(first, last)

    def wait_arrived():
        def wait_one(i, _):
            s = lax.rem(me + i, D)
            id_copy(s, s).wait_recv()
            row_copy(s, s).wait_recv()
            return 0

        lax.fori_loop(1, D, wait_one, 0)
        own_ids.wait()
        own_rows.wait()
        for g in range(groups):
            ids_g = ids_r[g * in_group]
            for i in range(1, in_group):
                ids_g = ids_g + ids_r[g * in_group + i]
            lr_ref[:, g * GROUP:(g + 1) * GROUP] = ids_g

    def placed(first, count):
        slots = lax.broadcasted_iota(jnp.int32, (count, rows_dev), 0) + first
        put = jnp.where(slots == lr_ref[...], 1.0, 0.0).astype(BF16)
        return dot(put, rv[...].reshape(rows_dev, draws))

    def piece(slot, c, q, send_sem, to_row, to_col):
        return pltpu.make_async_remote_copy(
            src_ref=H.at[slot, c, q], dst_ref=H.at[slot, c, q], send_sem=send_sem, recv_sem=p_recv.at[slot, c, q],
            device_id=(to_row, to_col), device_id_type=MESH)

    def slab(u, slot, c, i):
        return pltpu.make_async_remote_copy(
            src_ref=H.at[slot, c], dst_ref=H.at[slot, c], send_sem=d_send.at[u, i], recv_sem=d_recv.at[slot, c],
            device_id=(sibling, col), device_id_type=MESH)

    def share_out(u, slot, k):
        for q in range(1, nq):
            piece(slot, col, q, a_send.at[u, q], 2 * q + k, col).start()

    def share(u, slot, k, between):
        @pl.when(row != k)
        def _():
            piece(slot, col, quarter, a_send.at[u, 0], sibling, col).wait_recv()

        for i in range(1, C):
            other = lax.rem(col + i, C)
            piece(slot, col, quarter, b_send.at[u, i], row, other).start()
        for i in range(C):
            c = lax.rem(col + i, C)
            if i:
                piece(slot, c, quarter, b_send.at[u, i], sibling, col).wait_recv()
            for j in range(1, nq):
                q = lax.rem(quarter + j, nq)

                def go(c=c, q=q, i=i, j=j):
                    piece(slot, c, quarter, c_send.at[u, i, j], 2 * q + k, col).start()

                if i:
                    go()
                else:
                    pl.when(q != 0)(go)
            between()
        for i in range(C):
            c = lax.rem(col + i, C)
            for j in range(1, nq):
                q = lax.rem(quarter + j, nq)

                def take(c=c, q=q):
                    piece(slot, c, q, a_send.at[u, 0], sibling, col).wait_recv()

                if i:
                    take()
                else:
                    pl.when(row != k)(take)
            slab(u, slot, c, i).start()
            between()

    def received(slot):
        for c in range(C):
            slab(0, slot, c, 0).wait_recv()

    def settle(u, slot, k):
        @pl.when(row == k)
        def _():
            for q in range(1, nq):
                piece(slot, col, q, a_send.at[u, q], 2 * q + k, col).wait_send()

        for i in range(1, C):
            piece(slot, col, quarter, b_send.at[u, i], row, col).wait_send()
        for i in range(C):
            for j in range(1, nq):
                q = lax.rem(quarter + j, nq)

                def done(i=i, j=j):
                    piece(slot, col, quarter, c_send.at[u, i, j], sibling, col).wait_send()

                if i:
                    done()
                else:
                    pl.when(q != 0)(done)
            slab(u, slot, lax.rem(col + i, C), i).wait_send()

    def multiply(left, right, store):
        def step(i, _):
            at = pl.ds(pl.multiple_of(i * GROUP, GROUP), GROUP)
            store(at, dot(left(at), right))
            return 0

        lax.fori_loop(0, panel_width // GROUP, step, 0)

    lead, early, each = plan
    pan_copy.wait()

    @pl.when(row == 1)
    def _():
        H[2, col] = pan[0, 0].reshape(nq, sub, draws)
        share_out(0, 2, 1)

    lax.fori_loop(0, 1, pick_group, 0)
    sent = send_until(0, C)
    lax.fori_loop(1, 2, pick_group, 0)
    sent = send_until(sent, 2 * C)
    lax.fori_loop(2, R, pick_group, 0)
    sent = send_until(sent, sent + lead)

    @pl.when(core == 1)
    def _():
        share(0, 2, 1, lambda: None)

    sent = send_until(sent, sent + early)

    @pl.when(row < 2)
    def _():
        wait_arrived()
        H[core, col] = placed(0, block_rows).astype(BF16).reshape(nq, sub, draws)
        share_out(1, core, core)

    count = [sent]

    def more():
        count[0] = send_until(count[0], count[0] + each)

    share(1, core, core, more)
    sent = send_until(count[0], D)
    diag_copy.wait()

    @pl.when(core == 1)
    def _():
        received(0)

    def keep(k):
        def store(at, value):
            sol[k, at, :] = value.astype(BF16)
        return store

    def store_second(at, value):
        sec[at, :] = (sec[at, :].astype(F32) - value).astype(BF16)

    multiply(lambda at: dg[0, at, :], H[0].reshape(panel_width, draws), keep(0))

    @pl.when(core == 0)
    def _():
        received(2)
        received(1)

    sec[...] = H[1].reshape(panel_width, draws)
    fac[...] = H[2].reshape(panel_width, draws)
    multiply(lambda at: fac[at, :], sol[0], store_second)
    multiply(lambda at: dg[1, at, :], sec[...], keep(1))

    def trailing(i, _):
        acc[i] = dot(pan[0, i], sol[0]) + dot(pan[1, i], sol[1])
        return 0

    lax.fori_loop(0, L, trailing, 0)

    @pl.when(row >= 2)
    def _():
        wait_arrived()

    def finish(i, _):
        out_ref[i] = (placed(i * block_rows, block_rows) - acc[i]).astype(BF16)
        return 0

    lax.fori_loop(0, L, finish, 0)
    own = pl.ds(pl.multiple_of(col * block_rows, block_rows), block_rows)
    for k in range(2):
        @pl.when(row == k)
        def _(k=k):
            out_ref[0] = sol[k, own, :]

    def left(i, _):
        t = lax.rem(me + i, D)
        id_copy(t, me).wait_send()
        row_copy(t, me).wait_send()
        return 0

    lax.fori_loop(1, D, left, 0)

    @pl.when(core == 1)
    def _():
        settle(0, 2, 1)

    settle(1, core, core)


def kernel_per_device(b_ingest, source_point, panels, diag_inverse):
    R, C = lax.axis_size("row"), lax.axis_size("col")
    D = R * C
    _, L, _, block_rows, panel_width = panels.shape
    rows_dev, draws = b_ingest.shape
    per_peer = rows_dev // D
    nq = R // 2
    dma = pltpu.SemaphoreType.DMA
    vmem = pl.BlockSpec(memory_space=pltpu.VMEM)
    hbm = pl.BlockSpec(memory_space=pl.ANY)
    out = pl.pallas_call(
        functools.partial(kernel, R, C, panel_width, PLAN),
        out_shape=jax.ShapeDtypeStruct((L, block_rows, draws), BF16),
        in_specs=[vmem, vmem, hbm, hbm],
        out_specs=vmem,
        scratch_shapes=[
            pltpu.VMEM((D, per_peer, draws), BF16),
            pltpu.VMEM((D, per_peer, draws), BF16),
            pltpu.VMEM((D, 1, GROUP), jnp.int32),
            pltpu.VMEM((D, 1, GROUP), jnp.int32),
            pltpu.VMEM((1, rows_dev), jnp.int32),
            pltpu.VMEM((1, rows_dev), jnp.int32),
            pltpu.VMEM((2, L, block_rows, panel_width), BF16),
            pltpu.VMEM((2, panel_width, panel_width), BF16),
            pltpu.VMEM((3, C, nq, block_rows // nq, draws), BF16),
            pltpu.VMEM((2, panel_width, draws), BF16),
            pltpu.VMEM((panel_width, draws), BF16),
            pltpu.VMEM((panel_width, panel_width), BF16),
            pltpu.VMEM((L, block_rows, draws), F32),
            dma((2,)),
            dma((2,)),
            dma((D,)),
            dma((D,)),
            dma((D,)),
            dma((D,)),
            dma((2, nq)),
            dma((2, C)),
            dma((2, C, nq)),
            dma((2, C)),
            dma((3, C, nq)),
            dma((3, C)),
        ],
        compiler_params=pltpu.CompilerParams(
            collective_id=0, has_side_effects=True, vmem_limit_bytes=60 * 1024 * 1024
        ),
        cost_estimate=pl.CostEstimate(
            flops=4 * rows_dev * panel_width * draws * 2, bytes_accessed=20 * 1024 * 1024, transcendentals=0
        ),
    )(source_point.reshape(1, rows_dev), b_ingest, panels, diag_inverse)
    return out.reshape(L, 1, block_rows, draws)


def per_device(b_ingest, source_point, panels, diag_inverse):
    R, C = lax.axis_size("row"), lax.axis_size("col")
    rows_dev, draws = b_ingest.shape
    block_rows, panel_width = panels.shape[3:]
    per_peer = rows_dev // (R * C)
    fits = (
        R % 2 == 0 and R > 3 and C > 1 and panel_width == draws
        and per_peer % 16 == 0 and GROUP % per_peer == 0
        and rows_dev % GROUP == 0 and panel_width % GROUP == 0
        and block_rows % (R // 2 * 16) == 0 and rows_dev <= 64 * 256
        and rows_dev * (12 * draws + 4 * panel_width) + panel_width * (6 * panel_width + 12 * draws) <= 50 * 1024 * 1024
    )
    body = kernel_per_device if fits else plain_per_device
    return body(b_ingest, source_point, panels, diag_inverse)


def solution(mesh):
    return jax.shard_map(
        per_device,
        mesh=mesh,
        in_specs=(
            P(("row", "col"), None),
            P(("row", "col")),
            P(None, None, "row", "col", None),
            P(),
        ),
        out_specs=P(None, "row", "col", None),
        check_vma=False,
    )
```

```python
import functools

import jax
import jax.numpy as jnp
from jax import lax
from jax.experimental import pallas as pl
from jax.experimental.pallas import tpu as pltpu
from jax.sharding import PartitionSpec as P

MESH = pl.DeviceIdType.MESH
BF16 = jnp.bfloat16
F32 = jnp.float32
GROUP = 256


def broadcast(block, axis, owner):
    block = jnp.where(lax.axis_index(axis) == owner, block, jnp.zeros_like(block))
    return lax.psum(block, axis)


def plain_per_device(b_ingest, source_point, panels, diag_inverse):
    row_count = lax.axis_size("row")
    col_count = lax.axis_size("col")
    dev_count = row_count * col_count
    block_rows = panels.shape[3]
    panel_width = panels.shape[4]
    local_count = panels.shape[1]
    rows_dev = local_count * block_rows
    draw_count = b_ingest.shape[1]
    per_peer = rows_dev // dev_count
    owner_block = source_point // panel_width
    target = owner_block % row_count * col_count + source_point % panel_width // block_rows
    sort_keys = target * rows_dev + jnp.arange(rows_dev, dtype=jnp.int32)
    ordering = jnp.argsort(sort_keys)
    ordered = b_ingest[ordering]
    ordered_ids = source_point[ordering]
    arrived, arrived_ids = (
        lax.all_to_all(
            ordered.reshape(dev_count, per_peer, draw_count),
            ("row", "col"),
            split_axis=0,
            concat_axis=0,
            tiled=True,
        ),
        lax.all_to_all(
            ordered_ids.reshape(dev_count, per_peer),
            ("row", "col"),
            split_axis=0,
            concat_axis=0,
            tiled=True,
        ),
    )
    arrived = arrived.reshape(rows_dev, draw_count)
    arrived_ids = arrived_ids.reshape(rows_dev)
    arrived_block = arrived_ids // panel_width
    local_row = arrived_block // row_count * block_rows + arrived_ids % panel_width % block_rows
    resident = jnp.zeros((rows_dev, draw_count), jnp.bfloat16).at[local_row].set(arrived)
    running = resident.astype(jnp.float32)
    row_id = lax.axis_index("row")
    col_id = lax.axis_index("col")
    global_block = jnp.arange(rows_dev, dtype=jnp.int32) // block_rows * row_count + row_id
    solved = []
    for panel_index in range(2):
        factor_rows = panels[panel_index].reshape(rows_dev, panel_width)
        inverse = diag_inverse[panel_index]
        leading = running[:block_rows].astype(jnp.bfloat16)
        shared = broadcast(leading, "row", panel_index)
        full_solved = jnp.dot(
            inverse,
            lax.all_gather(shared, "col", axis=0, tiled=True),
            preferred_element_type=jnp.float32,
        ).astype(jnp.bfloat16)
        update = jnp.dot(factor_rows, full_solved, preferred_element_type=jnp.float32)
        own_solved = lax.dynamic_slice_in_dim(full_solved, col_id * block_rows, block_rows, 0)
        running = running - jnp.where((global_block > panel_index)[:, None], update, 0.0)
        solved.append(own_solved)
    result = running.astype(jnp.bfloat16)
    head_rows = result[:block_rows]
    head_rows = jnp.where(row_id == 0, solved[0], jnp.where(row_id == 1, solved[1], head_rows))
    result = jnp.concatenate([head_rows, result[block_rows:]], axis=0)
    return result.reshape(local_count, 1, block_rows, draw_count)


PLAN = (0, 8, 4)


def dot(a, b):
    return jnp.dot(a, b, preferred_element_type=F32)


def kernel(
    R, C, panel_width, plan, id_ref, b_ref, pan_hbm, diag_hbm, out_ref,
    bs, rv, ids_s, ids_r, rank_ref, lr_ref, pan, dg, H, sol, sec, fac, acc,
    local_sem, self_sem, s_send, s_recv, i_send, i_recv, a_send, b_send, c_send, d_send, p_recv, d_recv,
):
    D = R * C
    rows_dev, draws = b_ref.shape
    per_peer = rows_dev // D
    L = pan.shape[1]
    block_rows = pan.shape[2]
    nq = R // 2
    sub = block_rows // nq
    in_group = GROUP // per_peer
    groups = rows_dev // GROUP
    row = lax.axis_index("row")
    col = lax.axis_index("col")
    me = row * C + col
    core = lax.rem(row, 2)
    quarter = lax.div(row, 2)
    sibling = row + 1 - 2 * core

    pan_copy = pltpu.make_async_copy(pan_hbm.at[:, :, 0], pan, local_sem.at[0])
    diag_copy = pltpu.make_async_copy(diag_hbm, dg, local_sem.at[1])
    pan_copy.start()
    diag_copy.start()

    barrier = pltpu.get_barrier_semaphore()

    def greet(i, _):
        peer = lax.rem(me + i, D)
        pl.semaphore_signal(barrier, inc=1, device_id=(lax.div(peer, C), lax.rem(peer, C)), device_id_type=MESH)
        return 0

    lax.fori_loop(1, D, greet, 0)

    ids = id_ref[...]
    block = lax.div(ids, panel_width)
    offset = ids - block * panel_width
    local_block = lax.div(block, R)
    target_col = lax.div(offset, block_rows)
    target = (block - local_block * R) * C + target_col
    local_row = local_block * block_rows + offset - target_col * block_rows
    hits = jnp.where(lax.broadcasted_iota(jnp.int32, (D, rows_dev), 0) == target, 1.0, 0.0)
    chunks = [hits[:, g * GROUP:(g + 1) * GROUP] for g in range(groups)]
    upper = jnp.where(
        lax.broadcasted_iota(jnp.int32, (GROUP, GROUP), 0) < lax.broadcasted_iota(jnp.int32, (GROUP, GROUP), 1), 1.0, 0.0
    ).astype(BF16)
    before = dot(jnp.concatenate(chunks, axis=0).astype(BF16), upper)
    carry = jnp.zeros((D, 1), F32)
    for g in range(groups):
        part = chunks[g] * (before[g * D:(g + 1) * D] + carry)
        rank_ref[:, g * GROUP:(g + 1) * GROUP] = jnp.sum(part, axis=0, keepdims=True).astype(jnp.int32)
        carry = carry + jnp.sum(chunks[g], axis=1, keepdims=True)
    rank = rank_ref[...]
    place = target * per_peer + rank
    high = lax.div(local_row, 64)
    low = local_row - high * 64
    coded = jnp.concatenate([hits * high.astype(F32), hits * low.astype(F32)], axis=0).astype(BF16)
    lane = rank + lax.rem(me, in_group) * per_peer
    spread = jnp.where(lax.broadcasted_iota(jnp.int32, (GROUP, rows_dev), 0) == lane, 1.0, 0.0).astype(BF16)
    sent_ids = lax.dot_general(coded, spread, (((1,), (1,)), ((), ())), preferred_element_type=F32)
    sent_ids = (sent_ids[:D] * 64.0 + sent_ids[D:]).astype(jnp.int32)
    for t in range(D):
        ids_s[t] = sent_ids[t:t + 1]
    rank_ref[...] = place

    pl.semaphore_wait(barrier, D - 1)

    def row_copy(t, slot):
        return pltpu.make_async_remote_copy(
            src_ref=bs.at[t], dst_ref=rv.at[slot], send_sem=s_send.at[t], recv_sem=s_recv.at[slot],
            device_id=(lax.div(t, C), lax.rem(t, C)), device_id_type=MESH)

    def id_copy(t, slot):
        return pltpu.make_async_remote_copy(
            src_ref=ids_s.at[t], dst_ref=ids_r.at[slot], send_sem=i_send.at[t], recv_sem=i_recv.at[slot],
            device_id=(lax.div(t, C), lax.rem(t, C)), device_id_type=MESH)

    own_rows = pltpu.make_async_copy(bs.at[me], rv.at[me], self_sem.at[0])
    own_ids = pltpu.make_async_copy(ids_s.at[me], ids_r.at[me], self_sem.at[1])

    def group_of(i):
        return jnp.where(i < 2, i, 2 + lax.rem(i + row, R - 2))

    def pick_group(i, _):
        g = group_of(i)
        slots = lax.broadcasted_iota(jnp.int32, (C * per_peer, rows_dev), 0) + g * (C * per_peer)
        pick = jnp.where(slots == rank_ref[...], 1.0, 0.0).astype(BF16)
        picked = dot(pick, b_ref[...]).astype(BF16)
        bs[pl.ds(g * C, C)] = picked.reshape(C, per_peer, draws)
        return 0

    def send_one(n, _):
        t = group_of(lax.div(n, C)) * C + lax.rem(col + n, C)

        @pl.when(t != me)
        def _():
            id_copy(t, me).start()
            row_copy(t, me).start()

        @pl.when(t == me)
        def _():
            own_ids.start()
            own_rows.start()

        return 0

    def send_until(first, last):
        last = min(last, D)
        if first < last:
            lax.fori_loop(first, last, send_one, 0)
        return max(first, last)

    def wait_arrived():
        def wait_one(i, _):
            s = lax.rem(me + i, D)
            id_copy(s, s).wait_recv()
            row_copy(s, s).wait_recv()
            return 0

        lax.fori_loop(1, D, wait_one, 0)
        own_ids.wait()
        own_rows.wait()
        for g in range(groups):
            ids_g = ids_r[g * in_group]
            for i in range(1, in_group):
                ids_g = ids_g + ids_r[g * in_group + i]
            lr_ref[:, g * GROUP:(g + 1) * GROUP] = ids_g

    def placed(first, count):
        slots = lax.broadcasted_iota(jnp.int32, (count, rows_dev), 0) + first
        put = jnp.where(slots == lr_ref[...], 1.0, 0.0).astype(BF16)
        return dot(put, rv[...].reshape(rows_dev, draws))

    def piece(slot, c, q, send_sem, to_row, to_col):
        return pltpu.make_async_remote_copy(
            src_ref=H.at[slot, c, q], dst_ref=H.at[slot, c, q], send_sem=send_sem, recv_sem=p_recv.at[slot, c, q],
            device_id=(to_row, to_col), device_id_type=MESH)

    def slab(u, slot, c, i):
        return pltpu.make_async_remote_copy(
            src_ref=H.at[slot, c], dst_ref=H.at[slot, c], send_sem=d_send.at[u, i], recv_sem=d_recv.at[slot, c],
            device_id=(sibling, col), device_id_type=MESH)

    def share_out(u, slot, k):
        for q in range(1, nq):
            piece(slot, col, q, a_send.at[u, q], 2 * q + k, col).start()

    def share(u, slot, k, between):
        @pl.when(row != k)
        def _():
            piece(slot, col, quarter, a_send.at[u, 0], sibling, col).wait_recv()

        for i in range(1, C):
            other = lax.rem(col + i, C)
            piece(slot, col, quarter, b_send.at[u, i], row, other).start()
        for i in range(C):
            c = lax.rem(col + i, C)
            if i:
                piece(slot, c, quarter, b_send.at[u, i], sibling, col).wait_recv()
            for j in range(1, nq):
                q = lax.rem(quarter + j, nq)

                def go(c=c, q=q, i=i, j=j):
                    piece(slot, c, quarter, c_send.at[u, i, j], 2 * q + k, col).start()

                if i:
                    go()
                else:
                    pl.when(q != 0)(go)
            between()
        for i in range(C):
            c = lax.rem(col + i, C)
            for j in range(1, nq):
                q = lax.rem(quarter + j, nq)

                def take(c=c, q=q):
                    piece(slot, c, q, a_send.at[u, 0], sibling, col).wait_recv()

                if i:
                    take()
                else:
                    pl.when(row != k)(take)
            slab(u, slot, c, i).start()
            between()

    def received(slot):
        for c in range(C):
            slab(0, slot, c, 0).wait_recv()

    def settle(u, slot, k):
        @pl.when(row == k)
        def _():
            for q in range(1, nq):
                piece(slot, col, q, a_send.at[u, q], 2 * q + k, col).wait_send()

        for i in range(1, C):
            piece(slot, col, quarter, b_send.at[u, i], row, col).wait_send()
        for i in range(C):
            for j in range(1, nq):
                q = lax.rem(quarter + j, nq)

                def done(i=i, j=j):
                    piece(slot, col, quarter, c_send.at[u, i, j], sibling, col).wait_send()

                if i:
                    done()
                else:
                    pl.when(q != 0)(done)
            slab(u, slot, lax.rem(col + i, C), i).wait_send()

    def multiply(left, right, store):
        def step(i, _):
            at = pl.ds(pl.multiple_of(i * GROUP, GROUP), GROUP)
            store(at, dot(left(at), right))
            return 0

        lax.fori_loop(0, panel_width // GROUP, step, 0)

    lead, early, each = plan
    pan_copy.wait()

    @pl.when(row == 1)
    def _():
        H[2, col] = pan[0, 0].reshape(nq, sub, draws)
        share_out(0, 2, 1)

    lax.fori_loop(0, 1, pick_group, 0)
    sent = send_until(0, C)
    lax.fori_loop(1, 2, pick_group, 0)
    sent = send_until(sent, 2 * C)
    lax.fori_loop(2, R, pick_group, 0)
    sent = send_until(sent, sent + lead)

    @pl.when(core == 1)
    def _():
        share(0, 2, 1, lambda: None)

    sent = send_until(sent, sent + early)

    @pl.when(row < 2)
    def _():
        wait_arrived()
        H[core, col] = placed(0, block_rows).astype(BF16).reshape(nq, sub, draws)
        share_out(1, core, core)

    count = [sent]

    def more():
        count[0] = send_until(count[0], count[0] + each)

    share(1, core, core, more)
    sent = send_until(count[0], D)
    diag_copy.wait()

    @pl.when(core == 1)
    def _():
        received(0)

    def keep(k):
        def store(at, value):
            sol[k, at, :] = value.astype(BF16)
        return store

    def store_second(at, value):
        sec[at, :] = (sec[at, :].astype(F32) - value).astype(BF16)

    multiply(lambda at: dg[0, at, :], H[0].reshape(panel_width, draws), keep(0))

    def first_panel(i, _):
        acc[i] = dot(pan[0, i], sol[0])
        return 0

    lax.fori_loop(0, L, first_panel, 0)

    @pl.when(core == 0)
    def _():
        received(2)
        received(1)

    sec[...] = H[1].reshape(panel_width, draws)
    fac[...] = H[2].reshape(panel_width, draws)
    multiply(lambda at: fac[at, :], sol[0], store_second)
    multiply(lambda at: dg[1, at, :], sec[...], keep(1))

    def second_panel(i, _):
        acc[i] += dot(pan[1, i], sol[1])
        return 0

    lax.fori_loop(0, L, second_panel, 0)

    @pl.when(row >= 2)
    def _():
        wait_arrived()

    def finish(i, _):
        out_ref[i] = (placed(i * block_rows, block_rows) - acc[i]).astype(BF16)
        return 0

    lax.fori_loop(0, L, finish, 0)
    own = pl.ds(pl.multiple_of(col * block_rows, block_rows), block_rows)
    for k in range(2):
        @pl.when(row == k)
        def _(k=k):
            out_ref[0] = sol[k, own, :]

    def left(i, _):
        t = lax.rem(me + i, D)
        id_copy(t, me).wait_send()
        row_copy(t, me).wait_send()
        return 0

    lax.fori_loop(1, D, left, 0)

    @pl.when(core == 1)
    def _():
        settle(0, 2, 1)

    settle(1, core, core)


def kernel_per_device(b_ingest, source_point, panels, diag_inverse):
    R, C = lax.axis_size("row"), lax.axis_size("col")
    D = R * C
    _, L, _, block_rows, panel_width = panels.shape
    rows_dev, draws = b_ingest.shape
    per_peer = rows_dev // D
    nq = R // 2
    dma = pltpu.SemaphoreType.DMA
    vmem = pl.BlockSpec(memory_space=pltpu.VMEM)
    hbm = pl.BlockSpec(memory_space=pl.ANY)
    out = pl.pallas_call(
        functools.partial(kernel, R, C, panel_width, PLAN),
        out_shape=jax.ShapeDtypeStruct((L, block_rows, draws), BF16),
        in_specs=[vmem, vmem, hbm, hbm],
        out_specs=vmem,
        scratch_shapes=[
            pltpu.VMEM((D, per_peer, draws), BF16),
            pltpu.VMEM((D, per_peer, draws), BF16),
            pltpu.VMEM((D, 1, GROUP), jnp.int32),
            pltpu.VMEM((D, 1, GROUP), jnp.int32),
            pltpu.VMEM((1, rows_dev), jnp.int32),
            pltpu.VMEM((1, rows_dev), jnp.int32),
            pltpu.VMEM((2, L, block_rows, panel_width), BF16),
            pltpu.VMEM((2, panel_width, panel_width), BF16),
            pltpu.VMEM((3, C, nq, block_rows // nq, draws), BF16),
            pltpu.VMEM((2, panel_width, draws), BF16),
            pltpu.VMEM((panel_width, draws), BF16),
            pltpu.VMEM((panel_width, panel_width), BF16),
            pltpu.VMEM((L, block_rows, draws), F32),
            dma((2,)),
            dma((2,)),
            dma((D,)),
            dma((D,)),
            dma((D,)),
            dma((D,)),
            dma((2, nq)),
            dma((2, C)),
            dma((2, C, nq)),
            dma((2, C)),
            dma((3, C, nq)),
            dma((3, C)),
        ],
        compiler_params=pltpu.CompilerParams(
            collective_id=0, has_side_effects=True, vmem_limit_bytes=60 * 1024 * 1024
        ),
        cost_estimate=pl.CostEstimate(
            flops=4 * rows_dev * panel_width * draws * 2, bytes_accessed=20 * 1024 * 1024, transcendentals=0
        ),
    )(source_point.reshape(1, rows_dev), b_ingest, panels, diag_inverse)
    return out.reshape(L, 1, block_rows, draws)


def per_device(b_ingest, source_point, panels, diag_inverse):
    R, C = lax.axis_size("row"), lax.axis_size("col")
    rows_dev, draws = b_ingest.shape
    block_rows, panel_width = panels.shape[3:]
    per_peer = rows_dev // (R * C)
    fits = (
        R % 2 == 0 and R > 3 and C > 1 and panel_width == draws
        and per_peer % 16 == 0 and GROUP % per_peer == 0
        and rows_dev % GROUP == 0 and panel_width % GROUP == 0
        and block_rows % (R // 2 * 16) == 0 and rows_dev <= 64 * 256
        and rows_dev * (12 * draws + 4 * panel_width) + panel_width * (6 * panel_width + 12 * draws) <= 50 * 1024 * 1024
    )
    body = kernel_per_device if fits else plain_per_device
    return body(b_ingest, source_point, panels, diag_inverse)


def solution(mesh):
    return jax.shard_map(
        per_device,
        mesh=mesh,
        in_specs=(
            P(("row", "col"), None),
            P(("row", "col")),
            P(None, None, "row", "col", None),
            P(),
        ),
        out_specs=P(None, "row", "col", None),
        check_vma=False,
    )
```
